32 devices in a mesh: groups: 2 (over y), blk: 4 (over z), dp: 4 (over x, core).
Axes of the slice: x: 2, y: 2, z: 4, core: 2. Of those that a mesh axis runs over, the one named last changes fastest.
Arguments:
- inputs: bfloat16 [1024, 4096], P(('groups', 'dp'), 'blk'), parts along dimension 0, may hold values from -6 to 6
- out_grad: bfloat16 [1024, 4096], P(('groups', 'dp'), 'blk'), parts along dimension 0, may hold values from -6 to 6
- gate_blocks: bfloat16 [4, 4, 10, 128, 128], P('blk', 'dp'), may hold values from -0.5 to 0.5
- up_blocks: bfloat16 [4, 4, 10, 128, 128], P('blk', 'dp'), may hold values from -0.5 to 0.5
- down_blocks: bfloat16 [4, 4, 10, 128, 128], P('blk', 'dp'), may hold values from -0.25 to 0.25
- gate_slots: int32 [4, 4, 10], P('blk'), may hold values from 0 to 256, as said below
- up_slots: int32 [4, 4, 10], P('blk'), may hold values from 0 to 256, as said below
- down_slots: int32 [4, 4, 10], P('blk'), may hold values from 0 to 256, as said below
Outputs:
- input_grad: bfloat16 [1024, 4096], P(('groups', 'dp'), 'blk'), parts along dimension 0
- gate_grad: bfloat16 [8, 4, 10, 128, 128], P(('groups', 'blk'), 'dp'), parts along dimension 0
- up_grad: bfloat16 [8, 4, 10, 128, 128], P(('groups', 'blk'), 'dp'), parts along dimension 0
- down_grad: bfloat16 [8, 4, 10, 128, 128], P(('groups', 'blk'), 'dp'), parts along dimension 0
The draws below stay inside these ranges and needn't reach their ends.
There are 2 independent parts, one for each index of `groups`. The reference program is written for one: setup_inputs(seed, part) draws one part's arguments, and reference() takes and returns one part's arrays. A program takes and returns all parts, laid end to end along the dimension named above; an argument that names none is the same for every part. Nothing has to cross between parts.
Inputs may be any that keep to these rules, and one draw needn't show every extreme that they name: `gate_slots`: for each matrix and each [r, k], the entries of [r, k, :] that are below 256 come first and are distinct; the remaining slots hold 256. At most 10 kept blocks per matrix on one [r, k], and in every draw some [r, k] uses all 10 slots. `up_slots`: as for gate_slots. `down_slots`: as for gate_slots.
All inputs are finite; a program needn't handle non-finite values.
Results may differ from the reference program's by a relative error of at most 0.005.
Values may be sent and summed in bfloat16 or wider, within the bound.
No kernel may reach another device: no remote copies, remote signals or barrier semaphores. Data moves between devices by JAX's collectives and lax.ppermute only.
A program may use at most 320 MiB of HBM per device.

```python
import jax
import jax.numpy as jnp

D = 4096
FF = 16384
BLOCK = 128
CAP = 10
TOKENS = 512
LOCAL_BLOCKS = 256
N_BLK = 4
N_DP = 4


def draw_slot_list(key):
    devices = N_BLK * N_DP
    count_key, place_key, shuffle_key = jax.random.split(key, 3)
    counts = jax.random.randint(count_key, (devices,), CAP // 2, CAP + 1)
    ranking = jax.random.permutation(place_key, devices)
    counts = jnp.where(ranking == 0, CAP, counts)
    device_keys = jax.random.split(shuffle_key, devices)
    shuffled = jax.vmap(lambda single: jax.random.permutation(single, LOCAL_BLOCKS))(device_keys)[:, :CAP]
    filled = jnp.arange(CAP)[None, :] < counts[:, None]
    slot_ids = jnp.where(filled, shuffled, LOCAL_BLOCKS)
    return slot_ids.reshape(N_BLK, N_DP, CAP).astype(jnp.int32)


def draw_gate_slots(key, part):
    key = jax.random.fold_in(key, 11)
    return draw_slot_list(key)


def draw_up_slots(key, part):
    key = jax.random.fold_in(key, 23)
    return draw_slot_list(key)


def draw_down_slots(key, part):
    key = jax.random.fold_in(key, 37)
    return draw_slot_list(key)


def block_scale(key, shape, pieces, least, largest):
    gain = 1.0
    for axis_at, blocks in pieces:
        heights = jax.random.uniform(jax.random.fold_in(jax.random.fold_in(key, 6), axis_at), (blocks,), jnp.float32, least / len(pieces), largest / len(pieces))
        gain = gain * jnp.repeat(jnp.exp(heights), shape[axis_at] // blocks).reshape((-1,) + (1,) * (len(shape) - 1 - axis_at))
    return gain


def bell_draw(key, shape, scale, bound, cuts=(), kind=jnp.bfloat16):
    gain = block_scale(key, shape, cuts, -0.22, 0.18) if cuts else 1.0
    values = jax.random.normal(key, shape, jnp.float32) * scale * gain
    return jnp.minimum(jnp.maximum(values, -bound), bound).astype(kind)


def setup_inputs(seed: int = 0, part: int = 0) -> dict:
    keys = jax.random.split(jax.random.key(seed), 9)
    own_keys = jax.random.split(jax.random.fold_in(keys[8], part), 9)
    return {
        "inputs": bell_draw(own_keys[0], (TOKENS, D), 1.0, 6.0, ((0, 4), (1, 4))),
        "out_grad": bell_draw(own_keys[1], (TOKENS, D), 1.0, 6.0, ((0, 4), (1, 4))),
        "gate_blocks": bell_draw(keys[2], (N_BLK, N_DP, CAP, BLOCK, BLOCK), (D * 3 * CAP // (4 * LOCAL_BLOCKS)) ** -0.5, 0.5, ((0, 4), (1, 4))),
        "up_blocks": bell_draw(keys[3], (N_BLK, N_DP, CAP, BLOCK, BLOCK), (D * 3 * CAP // (4 * LOCAL_BLOCKS)) ** -0.5, 0.5, ((0, 4), (1, 4))),
        "down_blocks": bell_draw(keys[4], (N_BLK, N_DP, CAP, BLOCK, BLOCK), (FF * 3 * CAP // (4 * LOCAL_BLOCKS)) ** -0.5, 0.25, ((0, 4), (1, 4))),
        "gate_slots": draw_gate_slots(jax.random.fold_in(keys[8], 71), part),
        "up_slots": draw_up_slots(jax.random.fold_in(keys[8], 71), part),
        "down_slots": draw_down_slots(jax.random.fold_in(keys[8], 71), part),
    }


def block_layout(slot_ids):
    local_rows = D // (BLOCK * N_DP)
    local_cols = FF // (BLOCK * N_BLK)
    block_limit = local_rows * local_cols
    usable = slot_ids < block_limit
    clipped = jnp.minimum(slot_ids, block_limit - 1)
    row_ids = jnp.arange(N_DP, dtype=jnp.int32)[None, :, None] * local_rows + clipped // local_cols
    col_ids = jnp.arange(N_BLK, dtype=jnp.int32)[:, None, None] * local_cols + clipped % local_cols
    return usable, row_ids.astype(jnp.int32), col_ids.astype(jnp.int32)


def spread_blocks(blocks, usable, first_ids, second_ids, first_total, second_total):
    kept = blocks * usable[..., None, None].astype(blocks.dtype)
    grid = jnp.zeros((first_total, second_total, BLOCK, BLOCK), blocks.dtype)
    grid = grid.at[first_ids, second_ids].add(kept)
    return grid.transpose(0, 2, 1, 3).reshape(first_total * BLOCK, second_total * BLOCK)


def pick_blocks(dense, usable, first_ids, second_ids):
    tiles = dense.reshape(dense.shape[0] // BLOCK, BLOCK, dense.shape[1] // BLOCK, BLOCK)
    picked = tiles[first_ids, :, second_ids, :]
    return (picked * usable[..., None, None].astype(jnp.float32)).astype(jnp.bfloat16)


def reference(inputs, out_grad, gate_blocks, up_blocks, down_blocks, gate_slots, up_slots, down_slots):
    row_total = D // BLOCK
    col_total = FF // BLOCK
    gate_use, gate_row, gate_col = block_layout(gate_slots)
    up_use, up_row, up_col = block_layout(up_slots)
    down_use, down_row, down_col = block_layout(down_slots)
    gate_weight = spread_blocks(gate_blocks, gate_use, gate_row, gate_col, row_total, col_total)
    up_weight = spread_blocks(up_blocks, up_use, up_row, up_col, row_total, col_total)
    down_weight = spread_blocks(down_blocks, down_use, down_col, down_row, col_total, row_total)
    gate_pre = jnp.dot(inputs, gate_weight, preferred_element_type=jnp.float32)
    up_pre = jnp.dot(inputs, up_weight, preferred_element_type=jnp.float32)
    hidden_delta = jnp.dot(out_grad, down_weight.T, preferred_element_type=jnp.float32)
    sigmoid_gate = jax.nn.sigmoid(gate_pre)
    activated = gate_pre * sigmoid_gate
    hidden_act = (activated * up_pre).astype(jnp.bfloat16)
    gate_delta = (hidden_delta * up_pre * sigmoid_gate * (1.0 + gate_pre * (1.0 - sigmoid_gate))).astype(jnp.bfloat16)
    up_delta = (hidden_delta * activated).astype(jnp.bfloat16)
    input_grad = (jnp.dot(gate_delta, gate_weight.T, preferred_element_type=jnp.float32)
                  + jnp.dot(up_delta, up_weight.T, preferred_element_type=jnp.float32)).astype(jnp.bfloat16)
    gate_grad = pick_blocks(jnp.dot(inputs.T, gate_delta, preferred_element_type=jnp.float32), gate_use, gate_row, gate_col)
    up_grad = pick_blocks(jnp.dot(inputs.T, up_delta, preferred_element_type=jnp.float32), up_use, up_row, up_col)
    down_grad = pick_blocks(jnp.dot(hidden_act.T, out_grad, preferred_element_type=jnp.float32), down_use, down_col, down_row)
    return input_grad, gate_grad, up_grad, down_grad
```

```python
import functools

import jax
import jax.numpy as jnp
from jax import lax
from jax.experimental import pallas as pl
from jax.experimental.pallas import tpu as pltpu
from jax.sharding import PartitionSpec as P

BLOCK = 128
F32 = jnp.float32
BF16 = jnp.bfloat16
NN = (((1,), (0,)), ((), ()))
NT = (((1,), (1,)), ((), ()))


def line_pieces(x, axis):
    n = lax.axis_size(axis)
    to_right = [(i, i + 1) for i in range(n - 1)]
    to_left = [(i + 1, i) for i in range(n - 1)]
    pieces, offsets = [x], [0]
    rightward = leftward = x
    for step in range(1, n):
        rightward = lax.ppermute(rightward, axis, to_right)
        leftward = lax.ppermute(leftward, axis, to_left)
        pieces += [rightward, leftward]
        offsets += [-step, step]
    return pieces, offsets


def xor_swap(x, axis, bit):
    return lax.ppermute(x, axis, [(i, i ^ bit) for i in range(lax.axis_size(axis))])


def xor_gather(x, axis):
    n = lax.axis_size(axis)
    held = {0: x}
    bit = n // 2
    while bit:
        held.update({place ^ bit: xor_swap(piece, axis, bit) for place, piece in held.items()})
        bit //= 2
    return [held[place] for place in range(n)]


def compute_kernel(
    dims, offsets, where_ref, gate_ref, up_ref, down_ref, *refs
):
    n_dp, cap, row_count, col_count, shard_blocks, n_blk = dims
    n_pieces = len(offsets)
    x_refs, g_refs = refs[:n_pieces], refs[n_pieces : 2 * n_pieces]
    at = 2 * n_pieces
    w_refs = refs[at : at + n_dp]
    at += n_dp
    part_refs = refs[at : at + n_dp]
    at += n_dp
    far_refs = refs[at : at + n_blk - 1]
    at += n_blk - 1
    own_ref = refs[at]
    at += 1
    (xs, xt, gs, gate_acc, up_acc, down_acc, tmp, gate_delta, up_delta, act_t, feature_acc) = refs[at:]
    slot_refs = (gate_ref, up_ref, down_ref)
    me_blk, me_dp = where_ref[0], where_ref[1]
    limit = row_count * col_count

    for offset, x_ref, g_ref in zip(offsets, x_refs, g_refs):
        shard = me_blk + offset

        @pl.when((shard >= 0) & (shard < n_blk))
        def _():
            for b in range(shard_blocks):
                piece = x_ref[:, b * BLOCK : (b + 1) * BLOCK]
                xs[shard * shard_blocks + b] = piece
                xt[shard * shard_blocks + b] = piece.T
                gs[shard * shard_blocks + b] = g_ref[:, b * BLOCK : (b + 1) * BLOCK]

    for acc in (gate_acc, up_acc, down_acc):
        acc[...] = jnp.zeros_like(acc)
    feature_acc[...] = jnp.zeros_like(feature_acc)

    def place(matrix, owner, slot):
        entry = slot_refs[matrix][owner, slot]
        kept = jnp.minimum(entry, limit - 1)
        return entry < limit, owner * row_count + kept // col_count, kept % col_count

    for j in range(n_dp):
        owner = me_dp ^ j
        for matrix, source, acc, form in ((0, xs, gate_acc, NN), (1, xs, up_acc, NN), (2, gs, down_acc, NT)):
            for s in range(cap):
                _, row, _ = place(matrix, owner, s)
                tmp[s] = lax.dot_general(
                    source[row], w_refs[j][matrix * cap + s], form, preferred_element_type=F32
                )
            for s in range(cap):
                used, _, col = place(matrix, owner, s)
                acc[jnp.where(used, col, col_count)] += tmp[s]

    def deltas(c, _):
        gate, up, hidden = gate_acc[c], up_acc[c], down_acc[c]
        sig = jax.nn.sigmoid(gate)
        activated = gate * sig
        act_t[c] = (activated * up).astype(BF16).T
        gate_delta[c] = (hidden * up * sig * (1.0 + gate * (1.0 - sig))).astype(BF16)
        up_delta[c] = (hidden * activated).astype(BF16)
        return 0

    lax.fori_loop(0, col_count, deltas, 0)

    for j in range(n_dp):
        owner = me_dp ^ j
        for matrix, delta in ((0, gate_delta), (1, up_delta)):
            for s in range(cap):
                _, _, col = place(matrix, owner, s)
                tmp[s] = lax.dot_general(
                    delta[col], w_refs[j][matrix * cap + s], NT, preferred_element_type=F32
                )
            for s in range(cap):
                used, row, _ = place(matrix, owner, s)
                feature_acc[jnp.where(used, row, n_blk * shard_blocks)] += tmp[s]

    for b in range(shard_blocks):
        own_ref[:, b * BLOCK : (b + 1) * BLOCK] = feature_acc[me_blk * shard_blocks + b]
    for shift in range(1, n_blk):
        shard = lax.rem(me_blk + shift, n_blk)
        for b in range(shard_blocks):
            far_refs[shift - 1][:, b * BLOCK : (b + 1) * BLOCK] = feature_acc[
                shard * shard_blocks + b
            ].astype(BF16)

    for j in range(n_dp):
        owner = me_dp ^ j
        for matrix in range(3):
            for s in range(cap):
                used, row, col = place(matrix, owner, s)
                if matrix == 2:
                    left, right = act_t[col], gs[row]
                else:
                    left, right = xt[row], (gate_delta, up_delta)[matrix][col]
                product = lax.dot_general(left, right, NN, preferred_element_type=F32)
                part_refs[j][matrix * cap + s] = jnp.where(used, product, 0.0).astype(part_refs[j].dtype)


def shards(inputs, out_grad, gate_blocks, up_blocks, down_blocks, gate_slots, up_slots, down_slots):
    n_dp, n_blk = lax.axis_size("dp"), lax.axis_size("blk")
    tokens, width = inputs.shape
    cap = gate_blocks.shape[2]
    row_blocks = n_blk * width // BLOCK
    row_count = row_blocks // n_dp
    hidden = 16384 // n_blk
    col_count = hidden // BLOCK
    blocks = jnp.concatenate([gate_blocks[0, 0], up_blocks[0, 0], down_blocks[0, 0]])
    weights = xor_gather(blocks, "dp")
    x_pieces, offsets = line_pieces(inputs, "blk")
    g_pieces, _ = line_pieces(out_grad, "blk")
    where = jnp.stack([lax.axis_index("blk"), lax.axis_index("dp")]).astype(jnp.int32)
    vmem = pl.BlockSpec(memory_space=pltpu.VMEM)
    smem = pl.BlockSpec(memory_space=pltpu.SMEM)
    shard_blocks = width // BLOCK
    n_slots = 3 * cap
    dims = (n_dp, cap, row_count, col_count, shard_blocks, n_blk)
    sent_on = [F32 if j % 2 == 0 else BF16 for j in range(n_dp)]
    results = pl.pallas_call(
        functools.partial(compute_kernel, dims, offsets),
        out_shape=(
            [jax.ShapeDtypeStruct((n_slots, BLOCK, BLOCK), kind) for kind in sent_on]
            + [jax.ShapeDtypeStruct((tokens, width), BF16)] * (n_blk - 1)
            + [jax.ShapeDtypeStruct((tokens, width), F32)]
        ),
        in_specs=[smem] * 4 + [vmem] * (2 * len(offsets) + n_dp),
        out_specs=[vmem] * (n_dp + n_blk),
        scratch_shapes=[
            pltpu.VMEM((row_blocks, tokens, BLOCK), BF16),
            pltpu.VMEM((row_blocks, BLOCK, tokens), BF16),
            pltpu.VMEM((row_blocks, tokens, BLOCK), BF16),
            pltpu.VMEM((col_count + 1, tokens, BLOCK), F32),
            pltpu.VMEM((col_count + 1, tokens, BLOCK), F32),
            pltpu.VMEM((col_count + 1, tokens, BLOCK), F32),
            pltpu.VMEM((cap, tokens, BLOCK), F32),
            pltpu.VMEM((col_count, tokens, BLOCK), BF16),
            pltpu.VMEM((col_count, tokens, BLOCK), BF16),
            pltpu.VMEM((col_count, BLOCK, tokens), BF16),
            pltpu.VMEM((row_blocks + 1, tokens, BLOCK), F32),
        ],
        compiler_params=pltpu.CompilerParams(vmem_limit_bytes=52 * 1024 * 1024),
    )(where, gate_slots[0], up_slots[0], down_slots[0], *x_pieces, *g_pieces, *weights)

    parts, far, total = results[:n_dp], results[n_dp:-1], results[-1]
    for shift in range(1, n_blk):
        moved = lax.ppermute(
            far[shift - 1], "blk", [(i, (i + shift) % n_blk) for i in range(n_blk)]
        )
        total = total + moved.astype(F32)
    input_grad = total.astype(BF16)

    bit = 1
    while bit < n_dp:
        arrived = [
            xor_swap(parts[j + 1].astype(BF16), "dp", bit) for j in range(0, len(parts), 2)
        ]
        parts = [kept + other.astype(F32) for kept, other in zip(parts[::2], arrived)]
        bit *= 2
    grads = parts[0].astype(BF16).reshape(3, 1, 1, cap, BLOCK, BLOCK)
    return input_grad, grads[0], grads[1], grads[2]


def solution(mesh):
    in_specs = (
        P(("groups", "dp"), "blk"),
        P(("groups", "dp"), "blk"),
        P("blk", "dp", None, None, None),
        P("blk", "dp", None, None, None),
        P("blk", "dp", None, None, None),
        P("blk", None, None),
        P("blk", None, None),
        P("blk", None, None),
    )
    out_specs = (
        P(("groups", "dp"), "blk"),
        P(("groups", "blk"), "dp", None, None, None),
        P(("groups", "blk"), "dp", None, None, None),
        P(("groups", "blk"), "dp", None, None, None),
    )
    return jax.shard_map(shards, mesh=mesh, in_specs=in_specs, out_specs=out_specs, check_vma=False)
```

```python
import functools

import jax
import jax.numpy as jnp
from jax import lax
from jax.experimental import pallas as pl
from jax.experimental.pallas import tpu as pltpu
from jax.sharding import PartitionSpec as P

BLOCK = 128
FF = 16384
F32 = jnp.float32
BF16 = jnp.bfloat16
NN = (((1,), (0,)), ((), ()))
NT = (((1,), (1,)), ((), ()))
TN = (((0,), (0,)), ((), ()))
MIB = 1024 * 1024
LONGEST_RING = 8
EVEN_MIB, ODD_MIB, DELTA_MIB, INPUT_MIB, NEAR_MIB = 20, 24, 28, 16, 14
EVEN_COST, ODD_COST, DELTA_COST, INPUT_COST, NEAR_COST = 1, 1, 12, 12, 6


def rotate(x, axis, shift):
    n = lax.axis_size(axis)
    return lax.ppermute(x, axis, [(i, (i + shift) % n) for i in range(n)])


def xor_swap(x, axis, bit):
    return lax.ppermute(x, axis, [(i, i ^ bit) for i in range(lax.axis_size(axis))])


def ring_gather(x, g, axis, ready):
    n = lax.axis_size(axis)
    if n > LONGEST_RING:
        me = lax.axis_index(axis)
        return [
            [piece] + [
                lax.dynamic_index_in_dim(whole, (me - i + n) % n, 0, keepdims=False) for i in range(1, n)
            ]
            for piece, whole in ((x, lax.all_gather(x, axis)), (g, lax.all_gather(g, axis)))
        ]
    xs, gs = [x], [g]
    for step in range(1, n):
        xs.append(rotate(xs[-1], axis, 1))
        gs.append(rotate(after(gs[-1], *ready) if step == 2 else gs[-1], axis, 1))
    return xs, gs


def after(x, *others):
    return lax.optimization_barrier((x, *others))[0]


class Dims:
    def __init__(self, n_dp, n_blk, cap, tokens, width):
        self.n_dp, self.n_blk, self.cap, self.tokens, self.width = n_dp, n_blk, cap, tokens, width
        self.shard_blocks = width // BLOCK
        self.rows = n_blk * self.shard_blocks
        self.own_rows = self.rows // n_dp
        self.cols = FF // (BLOCK * n_blk)
        self.limit = self.own_rows * self.cols
        self.paired = self.own_rows == self.shard_blocks

    def here(self, meta):
        return meta[0], meta[1]

    def place(self, meta, matrix, owner, slot):
        entry = meta[2 + (matrix * self.n_dp + owner) * self.cap + slot]
        kept = jnp.minimum(entry, self.limit - 1)
        return entry < self.limit, owner * self.own_rows + kept // self.cols, kept % self.cols

    def spread(self, piece_ref, shard, target):
        for b in range(self.shard_blocks):
            target[shard * self.shard_blocks + b] = piece_ref[:, b * BLOCK : (b + 1) * BLOCK]


def block(d, group, matrix, slot):
    return group[0][matrix * d.cap + slot] if len(group) == 1 else group[matrix][slot]


def add_products(d, meta, matrix, owner, group, source, form, acc):
    for s in range(d.cap):
        used, row, col = d.place(meta, matrix, owner, s)
        acc[jnp.where(used, col, d.cols)] += lax.dot_general(
            source[row], block(d, group, matrix, s), form, preferred_element_type=F32
        )


def forward_products(d, meta, group, j, xs, gs, gate_acc, up_acc, hidden):
    me_blk, me_dp = d.here(meta)
    owner = me_dp ^ j
    add_products(d, meta, 0, owner, group, xs, NN, gate_acc)
    add_products(d, meta, 1, owner, group, xs, NN, up_acc)
    if d.paired:
        there = owner != shard_at(d, me_blk, d.n_blk - 1)
        pl.when(there)(functools.partial(add_products, d, meta, 2, owner, group, gs, NT, hidden))


def take_groups(refs, places):
    groups, at = {}, 0
    for j in places:
        size = 1 if j < 2 else 3
        groups[j] = refs[at : at + size]
        at += size
    return groups, refs[at:]


def shard_at(d, me, i):
    return lax.rem(me - i + d.n_blk, d.n_blk)


def even_kernel(d, meta, own_ref, *refs):
    x_refs, g_refs = refs[: d.n_blk - 1], refs[d.n_blk - 1 : 2 * d.n_blk - 3]
    groups, outs = take_groups(refs[2 * d.n_blk - 3 :], range(0, d.n_dp, 2))
    xs, gs, gate_acc, up_acc, hidden = outs
    me_blk, _ = d.here(meta)
    own_x, own_g = own_ref.at[0], own_ref.at[1]
    for i, x_ref in enumerate((own_x, *x_refs)):
        d.spread(x_ref, shard_at(d, me_blk, i), xs)
    for i, g_ref in enumerate((own_g, *g_refs)):
        d.spread(g_ref, shard_at(d, me_blk, i), gs)
    for acc in (gate_acc, up_acc, hidden):
        acc[...] = jnp.zeros_like(acc)
    for j, group in groups.items():
        forward_products(d, meta, group, j, xs, gs, gate_acc, up_acc, hidden)


def odd_kernel(d, meta, xs, gs, gate_even, up_even, *refs):
    groups, outs = take_groups(refs, range(1, d.n_dp, 2))
    gate_slope, up_slope, act, hidden, gate_acc, up_acc = outs
    for acc in (gate_acc, up_acc, hidden):
        acc[...] = jnp.zeros_like(acc)
    for j, group in groups.items():
        forward_products(d, meta, group, j, xs, gs, gate_acc, up_acc, hidden)

    def activation(c, _):
        gate, up = gate_even[c] + gate_acc[c], up_even[c] + up_acc[c]
        sig = jax.nn.sigmoid(gate)
        activated = gate * sig
        act[c] = (activated * up).astype(BF16)
        gate_slope[c] = up * sig * (1.0 + gate * (1.0 - sig))
        up_slope[c] = activated
        return 0

    lax.fori_loop(0, d.cols, activation, 0)


def partial_grads(d, j, meta, xs, gs, act, gate_delta, up_delta, out_ref):
    owner = meta[1] ^ j
    for matrix in (2, 0, 1):
        for s in range(d.cap):
            used, row, col = d.place(meta, matrix, owner, s)
            if matrix == 2:
                left, right = act[col], gs[row]
            else:
                left, right = xs[row], (gate_delta, up_delta)[matrix][col]
            product = lax.dot_general(left, right, TN, preferred_element_type=F32)
            out_ref[matrix * d.cap + s] = jnp.where(used, product, 0.0).astype(out_ref.dtype)


def delta_kernel(d, places, meta, xs, gs_early, act, gate_slope, up_slope, hidden_even, hidden_odd, g_ref, *refs):
    groups, outs = take_groups(refs, range(d.n_dp))
    gate_delta, up_delta, gs = outs[:3]
    part_refs, more = outs[3:-1], outs[-1]
    me_blk, me_dp = d.here(meta)
    last = shard_at(d, me_blk, d.n_blk - 1)
    gs[...] = gs_early[...]
    d.spread(g_ref, last, gs)
    more[...] = jnp.zeros_like(more)
    for j in range(d.n_dp):
        owner = me_dp ^ j
        late = functools.partial(add_products, d, meta, 2, owner, groups[j], gs, NT, more)
        if d.paired:
            pl.when(owner == last)(late)
        else:
            late()

    def deltas(c, _):
        total = (hidden_even[c] + hidden_odd[c]) + more[c]
        gate_delta[c] = (total * gate_slope[c]).astype(BF16)
        up_delta[c] = (total * up_slope[c]).astype(BF16)
        return 0

    lax.fori_loop(0, d.cols, deltas, 0)
    for j, part_ref in zip(places, part_refs):
        partial_grads(d, j, meta, xs, gs, act, gate_delta, up_delta, part_ref)


def input_kernel(d, meta, gate_delta, up_delta, *refs):
    groups, outs = take_groups(refs, range(d.n_dp))
    out_refs, acc = outs[:-1], outs[-1]
    me_blk, me_dp = d.here(meta)
    acc[...] = jnp.zeros_like(acc)
    for j in range(d.n_dp):
        owner = me_dp ^ j
        for matrix, delta in ((0, gate_delta), (1, up_delta)):
            for s in range(d.cap):
                used, row, col = d.place(meta, matrix, owner, s)
                acc[jnp.where(used, row, d.rows)] += lax.dot_general(
                    delta[col], block(d, groups[j], matrix, s), NT, preferred_element_type=F32
                )
    for shift, out_ref in enumerate(out_refs):
        shard = lax.rem(me_blk + shift, d.n_blk)
        for b in range(d.shard_blocks):
            out_ref[:, b * BLOCK : (b + 1) * BLOCK] = acc[shard * d.shard_blocks + b].astype(out_ref.dtype)


def near_kernel(d, places, meta, xs, gs, act, gate_delta, up_delta, *part_refs):
    for j, part_ref in zip(places, part_refs):
        partial_grads(d, j, meta, xs, gs, act, gate_delta, up_delta, part_ref)


def call(kernel, outs, scratch, mib, cost, meta, *operands):
    vmem = pl.BlockSpec(memory_space=pltpu.VMEM)
    return pl.pallas_call(
        kernel,
        out_shape=outs,
        in_specs=[pl.BlockSpec(memory_space=pltpu.SMEM)] + [vmem] * len(operands),
        out_specs=[vmem] * len(outs),
        scratch_shapes=scratch,
        compiler_params=pltpu.CompilerParams(vmem_limit_bytes=mib * MIB),
        cost_estimate=pl.CostEstimate(flops=MIB, bytes_accessed=cost * MIB, transcendentals=0),
    )(meta, *operands)


def shards(inputs, out_grad, gate_blocks, up_blocks, down_blocks, gate_slots, up_slots, down_slots):
    n_dp, n_blk = lax.axis_size("dp"), lax.axis_size("blk")
    tokens, width = inputs.shape
    cap = gate_blocks.shape[2]
    d = Dims(n_dp, n_blk, cap, tokens, width)
    where = jnp.stack([lax.axis_index("blk"), lax.axis_index("dp")]).astype(jnp.int32)
    meta = jnp.concatenate([where] + [slots.reshape(-1) for slots in (gate_slots, up_slots, down_slots)])
    own_pair = jnp.stack([inputs, out_grad])

    matrices = [blocks[0, 0] for blocks in (gate_blocks, up_blocks, down_blocks)]
    groups = {0: [jnp.concatenate(matrices)]}
    groups[1] = [xor_swap(groups[0][0], "dp", 1)]
    x_pieces, g_pieces = ring_gather(inputs, out_grad, "blk", (own_pair, groups[0][0], groups[1][0], meta))
    bit = 2
    while bit < n_dp:
        for j in range(0, bit, 2):
            groups[j ^ bit] = [xor_swap(x, "dp", bit) for x in (groups[j] if j else matrices)]
        bit *= 2
    for j in range(2, n_dp, 2):
        groups[j + 1] = [xor_swap(after(x, *x_pieces[-2:-1]), "dp", 1) for x in groups[j]]

    def grid(count, kind):
        return jax.ShapeDtypeStruct((count, tokens, BLOCK), kind)

    def part(j):
        return jax.ShapeDtypeStruct((3 * cap, BLOCK, BLOCK), BF16 if j % 2 else F32)

    def blocks_at(places):
        return [x for j in places for x in groups[j]]

    sums = [grid(d.cols + 1, F32)] * 3
    xs, gs, gate_even, up_even, hidden_even = call(
        functools.partial(even_kernel, d), [grid(d.rows, BF16)] * 2 + sums, [], EVEN_MIB, EVEN_COST,
        meta, own_pair, *x_pieces[1:], *g_pieces[1:-1], *blocks_at(range(0, n_dp, 2)),
    )
    gate_slope, up_slope, act, hidden_odd = call(
        functools.partial(odd_kernel, d),
        [grid(d.cols, F32), grid(d.cols, F32), grid(d.cols, BF16), grid(d.cols + 1, F32)],
        [pltpu.VMEM((d.cols + 1, tokens, BLOCK), F32)] * 2, ODD_MIB, ODD_COST,
        meta, xs, gs, gate_even, up_even, *blocks_at(range(1, n_dp, 2)),
    )
    later = list(range(n_dp - 1, 1, -1))
    gate_delta, up_delta, gs, *parts_later = call(
        functools.partial(delta_kernel, d, later),
        [grid(d.cols, BF16), grid(d.cols, BF16), grid(d.rows, BF16)] + [part(j) for j in later],
        [pltpu.VMEM((d.cols + 1, tokens, BLOCK), F32)],
        DELTA_MIB, DELTA_COST, meta, xs, gs, act, gate_slope, up_slope, hidden_even, hidden_odd,
        g_pieces[-1], *blocks_at(range(n_dp)),
    )
    own, *far = call(
        functools.partial(input_kernel, d),
        [jax.ShapeDtypeStruct((tokens, width), F32)] + [jax.ShapeDtypeStruct((tokens, width), BF16)] * (n_blk - 1),
        [pltpu.VMEM((d.rows + 1, tokens, BLOCK), F32)],
        INPUT_MIB, INPUT_COST, meta, gate_delta, up_delta, *blocks_at(range(n_dp)),
    )
    near = [1, 0]
    parts_near = call(
        functools.partial(near_kernel, d, near),
        [part(j) for j in near], [], NEAR_MIB, NEAR_COST, meta, xs, gs, act, gate_delta, up_delta,
    )
    by_place = dict(zip(later + near, [*parts_later, *parts_near]))
    parts = [by_place[j] for j in range(n_dp)]

    bit = 1
    while bit < n_dp:
        arrived = [xor_swap(parts[j + 1].astype(BF16), "dp", bit) for j in range(0, len(parts), 2)]
        kept = parts[::2]
        bit *= 2
        if bit < n_dp:
            parts = [a + b.astype(F32) for a, b in zip(kept, arrived)]
    grads = [
        (kept[0][m * cap : (m + 1) * cap] + arrived[0][m * cap : (m + 1) * cap].astype(F32))
        .astype(BF16)
        .reshape(1, 1, cap, BLOCK, BLOCK)
        for m in range(3)
    ]
    for shift in range(1, n_blk):
        own = own + rotate(far[shift - 1], "blk", shift).astype(F32)
    return own.astype(BF16), *grads


def solution(mesh):
    in_specs = (
        P(("groups", "dp"), "blk"),
        P(("groups", "dp"), "blk"),
        P("blk", "dp", None, None, None),
        P("blk", "dp", None, None, None),
        P("blk", "dp", None, None, None),
        P("blk", None, None),
        P("blk", None, None),
        P("blk", None, None),
    )
    out_specs = (
        P(("groups", "dp"), "blk"),
        P(("groups", "blk"), "dp", None, None, None),
        P(("groups", "blk"), "dp", None, None, None),
        P(("groups", "blk"), "dp", None, None, None),
    )
    return jax.shard_map(shards, mesh=mesh, in_specs=in_specs, out_specs=out_specs, check_vma=False)
```

```python
import functools

import jax
import jax.numpy as jnp
from jax import lax
from jax.experimental import pallas as pl
from jax.experimental.pallas import tpu as pltpu
from jax.sharding import PartitionSpec as P

BLOCK = 128
FF = 16384
F32 = jnp.float32
BF16 = jnp.bfloat16
NN = (((1,), (0,)), ((), ()))
NT = (((1,), (1,)), ((), ()))
TN = (((0,), (0,)), ((), ()))
MIB = 1024 * 1024
LONGEST_RING = 8
PIECES = 2
EARLY_MIB, LATE_MIB, DELTA_MIB, INPUT_MIB, NEAR_MIB = 18, 22, 28, 16, 14
EARLY_COST, LATE_COST, DELTA_COST, INPUT_COST, NEAR_COST = 8, 8, 8, 8, 8


def rotate(x, axis, shift):
    n = lax.axis_size(axis)
    return lax.ppermute(x, axis, [(i, (i + shift) % n) for i in range(n)])


def xor_swap(x, axis, bit):
    return lax.ppermute(x, axis, [(i, i ^ bit) for i in range(lax.axis_size(axis))])


def ring_gather(x, g, axis, hold):
    n = lax.axis_size(axis)
    if n > LONGEST_RING:
        me = lax.axis_index(axis)
        return [
            [own] + [lax.dynamic_index_in_dim(whole, (me - i + n) % n, 0, keepdims=False) for i in range(1, n)]
            for own, whole in ((x, lax.all_gather(x, axis)), (g, lax.all_gather(g, axis)))
        ]
    xs, gs = [x], [g]
    for hop in range(1, n):
        xs.append(rotate(xs[-1], axis, 1))
        gs.append(rotate(after(gs[-1], *hold) if hop == 2 else gs[-1], axis, 1))
    return xs, gs


def after(x, *others):
    return lax.optimization_barrier((x, *others))[0]


class Dims:
    def __init__(self, n_dp, n_blk, cap, tokens, width):
        self.n_dp, self.n_blk, self.cap, self.tokens, self.width = n_dp, n_blk, cap, tokens, width
        self.shard_blocks = width // BLOCK
        self.rows = n_blk * self.shard_blocks
        self.own_rows = self.rows // n_dp
        self.cols = FF // (BLOCK * n_blk)
        self.limit = self.own_rows * self.cols
        self.paired = self.own_rows == self.shard_blocks

    def here(self, meta):
        return meta[0], meta[1]

    def place(self, meta, matrix, owner, slot):
        entry = meta[2 + (matrix * self.n_dp + owner) * self.cap + slot]
        kept = jnp.minimum(entry, self.limit - 1)
        return entry < self.limit, owner * self.own_rows + kept // self.cols, kept % self.cols

    def spread(self, piece_ref, shard, target):
        for b in range(self.shard_blocks):
            target[shard * self.shard_blocks + b] = piece_ref[:, b * BLOCK : (b + 1) * BLOCK]


def block(d, group, matrix, slot):
    return group[0][matrix * d.cap + slot] if len(group) == 1 else group[matrix][slot]


def add_products(d, meta, matrix, owner, group, source, form, acc):
    for s in range(d.cap):
        used, row, col = d.place(meta, matrix, owner, s)
        acc[jnp.where(used, col, d.cols)] += lax.dot_general(
            source[row], block(d, group, matrix, s), form, preferred_element_type=F32
        )


def take_groups(refs, places):
    groups, at = {}, 0
    for j in places:
        size = 3 if j else 1
        groups[j] = refs[at : at + size]
        at += size
    return groups, refs[at:]


def shard_at(d, me, i):
    return lax.rem(me - i + d.n_blk, d.n_blk)


def spread_all(d, me, refs, target):
    for i, ref in enumerate(refs):
        d.spread(ref, shard_at(d, me, i), target)


def early_kernel(d, meta, own_ref, *refs):
    x_refs, g_refs = refs[: d.n_blk - 2], refs[d.n_blk - 2 : 2 * d.n_blk - 4]
    groups, outs = take_groups(refs[2 * d.n_blk - 4 :], range(d.n_dp))
    gate_acc, up_acc, hidden, xs, gs = outs
    me_blk, me_dp = d.here(meta)
    for acc in (gate_acc, up_acc, hidden):
        acc[...] = jnp.zeros_like(acc)
    if not d.paired:
        return
    spread_all(d, me_blk, (own_ref.at[0], *x_refs), xs)
    spread_all(d, me_blk, (own_ref.at[1], *g_refs), gs)
    for j, group in groups.items():
        owner = me_dp ^ j

        @pl.when(owner != shard_at(d, me_blk, d.n_blk - 1))
        def _():
            add_products(d, meta, 0, owner, group, xs, NN, gate_acc)
            add_products(d, meta, 1, owner, group, xs, NN, up_acc)
            add_products(d, meta, 2, owner, group, gs, NT, hidden)


def when_late(d, meta, owner, work):
    if d.paired:
        pl.when(owner == shard_at(d, meta[0], d.n_blk - 1))(work)
    else:
        work()


def late_kernel(d, meta, own_ref, *refs):
    x_refs, (gate_early, up_early) = refs[: d.n_blk - 1], refs[d.n_blk - 1 : d.n_blk + 1]
    groups, outs = take_groups(refs[d.n_blk + 1 :], range(d.n_dp))
    gate_slope, up_slope, act, xs, gate_acc, up_acc = outs
    me_blk, me_dp = d.here(meta)
    for acc in (gate_acc, up_acc):
        acc[...] = jnp.zeros_like(acc)
    spread_all(d, me_blk, (own_ref.at[0], *x_refs), xs)
    for j, group in groups.items():
        owner = me_dp ^ j

        def work():
            add_products(d, meta, 0, owner, group, xs, NN, gate_acc)
            add_products(d, meta, 1, owner, group, xs, NN, up_acc)

        when_late(d, meta, owner, work)

    def activation(c, _):
        gate, up = gate_early[c] + gate_acc[c], up_early[c] + up_acc[c]
        sig = jax.nn.sigmoid(gate)
        activated = gate * sig
        act[c] = (activated * up).astype(BF16)
        gate_slope[c] = up * sig * (1.0 + gate * (1.0 - sig))
        up_slope[c] = activated
        return 0

    lax.fori_loop(0, d.cols, activation, 0, unroll=4)


def partial_grads(d, j, meta, xs, gs, act, gate_delta, up_delta, out_ref):
    owner = meta[1] ^ j
    for matrix in (2, 0, 1):
        for s in range(d.cap):
            used, row, col = d.place(meta, matrix, owner, s)
            if matrix == 2:
                left, right = act[col], gs[row]
            else:
                left, right = xs[row], (gate_delta, up_delta)[matrix][col]
            product = lax.dot_general(left, right, TN, preferred_element_type=F32)
            out_ref[matrix * d.cap + s] = jnp.where(used, product, 0.0).astype(out_ref.dtype)


def delta_kernel(d, places, meta, own_ref, xs, act, gate_slope, up_slope, hidden, *refs):
    g_refs = refs[: d.n_blk - 1]
    groups, outs = take_groups(refs[d.n_blk - 1 :], range(d.n_dp))
    gate_delta, up_delta, gs = outs[:3]
    part_refs, more = outs[3:-1], outs[-1]
    me_blk, me_dp = d.here(meta)
    more[...] = jnp.zeros_like(more)
    spread_all(d, me_blk, (own_ref.at[1], *g_refs), gs)
    for j, group in groups.items():
        owner = me_dp ^ j
        when_late(d, meta, owner, functools.partial(add_products, d, meta, 2, owner, group, gs, NT, more))

    def deltas(c, _):
        total = hidden[c] + more[c]
        gate_delta[c] = (total * gate_slope[c]).astype(BF16)
        up_delta[c] = (total * up_slope[c]).astype(BF16)
        return 0

    lax.fori_loop(0, d.cols, deltas, 0, unroll=4)
    for j, part_ref in zip(places, part_refs):
        partial_grads(d, j, meta, xs, gs, act, gate_delta, up_delta, part_ref)


def input_kernel(d, meta, gate_delta, up_delta, *refs):
    groups, outs = take_groups(refs, range(d.n_dp))
    out_refs, acc = outs[:-1], outs[-1]
    me_blk, me_dp = d.here(meta)
    acc[...] = jnp.zeros_like(acc)
    for j in range(d.n_dp):
        owner = me_dp ^ j
        for matrix, delta in ((0, gate_delta), (1, up_delta)):
            for s in range(d.cap):
                used, row, col = d.place(meta, matrix, owner, s)
                acc[jnp.where(used, row, d.rows)] += lax.dot_general(
                    delta[col], block(d, groups[j], matrix, s), NT, preferred_element_type=F32
                )
    for shift, out_ref in enumerate(out_refs):
        shard = lax.rem(me_blk + shift, d.n_blk)
        for b in range(d.shard_blocks):
            out_ref[:, b * BLOCK : (b + 1) * BLOCK] = acc[shard * d.shard_blocks + b].astype(out_ref.dtype)


class Pieces:
    def __init__(self, refs):
        self.refs, self.size, self.dtype = refs, refs[0].shape[0], refs[0].dtype

    def __setitem__(self, at, value):
        self.refs[at // self.size][at % self.size] = value


def near_kernel(d, meta, xs, gs, act, gate_delta, up_delta, own_ref, *next_refs):
    for j, part_ref in ((1, Pieces(next_refs)), (0, own_ref)):
        partial_grads(d, j, meta, xs, gs, act, gate_delta, up_delta, part_ref)


def call(kernel, outs, scratch, mib, cost, meta, *operands):
    vmem = pl.BlockSpec(memory_space=pltpu.VMEM)
    return pl.pallas_call(
        kernel,
        out_shape=outs,
        in_specs=[pl.BlockSpec(memory_space=pltpu.SMEM)] + [vmem] * len(operands),
        out_specs=[vmem] * len(outs),
        scratch_shapes=scratch,
        compiler_params=pltpu.CompilerParams(vmem_limit_bytes=mib * MIB),
        cost_estimate=pl.CostEstimate(flops=MIB, bytes_accessed=cost * MIB, transcendentals=0),
    )(meta, *operands)


def shards(inputs, out_grad, gate_blocks, up_blocks, down_blocks, gate_slots, up_slots, down_slots):
    n_dp, n_blk = lax.axis_size("dp"), lax.axis_size("blk")
    tokens, width = inputs.shape
    cap = gate_blocks.shape[2]
    d = Dims(n_dp, n_blk, cap, tokens, width)
    where = jnp.stack([lax.axis_index("blk"), lax.axis_index("dp")]).astype(jnp.int32)
    meta = jnp.concatenate([where] + [slots.reshape(-1) for slots in (gate_slots, up_slots, down_slots)])
    own_pair = jnp.stack([inputs, out_grad])

    matrices = [blocks[0, 0] for blocks in (gate_blocks, up_blocks, down_blocks)]
    groups = {0: [jnp.concatenate(matrices)], 1: [xor_swap(x, "dp", 1) for x in matrices]}
    own = (own_pair, groups[0][0], meta)
    bit = 2
    while bit < n_dp:
        for j in range(0, bit, 2):
            gate, up, down = groups[j] if j else matrices
            gate = xor_swap(after(gate, *groups[1]), "dp", bit)
            up = xor_swap(after(up, *own), "dp", bit)
            down = xor_swap(after(down, gate), "dp", bit)
            groups[j ^ bit] = [gate, up, down]
        bit *= 2
    x_pieces, g_pieces = ring_gather(inputs, out_grad, "blk", (*own, *groups[1]))
    for j in range(2, n_dp, 2):
        groups[j + 1] = [xor_swap(after(x, x_pieces[-2]), "dp", 1) for x in groups[j]]

    def grid(count, kind):
        return jax.ShapeDtypeStruct((count, tokens, BLOCK), kind)

    def part(j):
        return jax.ShapeDtypeStruct((3 * cap, BLOCK, BLOCK), BF16 if j % 2 else F32)

    def blocks_at(places):
        return [x for j in places for x in groups[j]]

    everyone = blocks_at(range(n_dp))
    sums = [grid(d.cols + 1, F32)] * 3
    gate_early, up_early, hidden = call(
        functools.partial(early_kernel, d), sums, [pltpu.VMEM((d.rows, tokens, BLOCK), BF16)] * 2, EARLY_MIB, EARLY_COST,
        meta, own_pair, *x_pieces[1:-1], *g_pieces[1:-1], *everyone,
    )
    gate_slope, up_slope, act, xs = call(
        functools.partial(late_kernel, d),
        [grid(d.cols, F32), grid(d.cols, F32), grid(d.cols, BF16), grid(d.rows, BF16)],
        [pltpu.VMEM((d.cols + 1, tokens, BLOCK), F32)] * 2, LATE_MIB, LATE_COST,
        meta, own_pair, *x_pieces[1:], gate_early, up_early, *everyone,
    )
    later = list(range(n_dp - 1, 1, -1))
    gate_delta, up_delta, gs, *parts_later = call(
        functools.partial(delta_kernel, d, later),
        [grid(d.cols, BF16), grid(d.cols, BF16), grid(d.rows, BF16)] + [part(j) for j in later],
        [pltpu.VMEM((d.cols + 1, tokens, BLOCK), F32)],
        DELTA_MIB, DELTA_COST, meta, own_pair, xs, act, gate_slope, up_slope, hidden, *g_pieces[1:], *everyone,
    )
    own, *far = call(
        functools.partial(input_kernel, d),
        [jax.ShapeDtypeStruct((tokens, width), F32)] + [jax.ShapeDtypeStruct((tokens, width), BF16)] * (n_blk - 1),
        [pltpu.VMEM((d.rows + 1, tokens, BLOCK), F32)],
        INPUT_MIB, INPUT_COST, meta, gate_delta, up_delta, *everyone,
    )
    far_parts = dict(zip(later, parts_later))

    relayed = []
    for j in range(2, n_dp, 2):
        other = xor_swap(far_parts[j + 1], "dp", 1)
        relayed.append(far_parts[j] + after(other, *far).astype(F32))
    moved = [rotate(far[shift - 1], "blk", shift) for shift in range(1, n_blk)]
    part_own, *parts_next = call(
        functools.partial(near_kernel, d),
        [part(0)] + [jax.ShapeDtypeStruct((3 * cap // PIECES, BLOCK, BLOCK), BF16)] * PIECES,
        [], NEAR_MIB, NEAR_COST, meta, xs, gs, act, after(gate_delta, *relayed), up_delta,
    )
    part_own = part_own + jnp.concatenate([xor_swap(piece, "dp", 1) for piece in parts_next]).astype(F32)
    parts = [part_own, *relayed]
    bit = 2
    while bit < n_dp:
        arrived = [xor_swap(parts[j + 1].astype(BF16), "dp", bit) for j in range(0, len(parts), 2)]
        kept = parts[::2]
        bit *= 2
        if bit < n_dp:
            parts = [a + b.astype(F32) for a, b in zip(kept, arrived)]
    grads = [
        (kept[0][m * cap : (m + 1) * cap] + arrived[0][m * cap : (m + 1) * cap].astype(F32))
        .astype(BF16)
        .reshape(1, 1, cap, BLOCK, BLOCK)
        for m in range(3)
    ]
    for piece in moved:
        own = own + piece.astype(F32)
    return own.astype(BF16), *grads


def solution(mesh):
    in_specs = (
        P(("groups", "dp"), "blk"),
        P(("groups", "dp"), "blk"),
        P("blk", "dp", None, None, None),
        P("blk", "dp", None, None, None),
        P("blk", "dp", None, None, None),
        P("blk", None, None),
        P("blk", None, None),
        P("blk", None, None),
    )
    out_specs = (
        P(("groups", "dp"), "blk"),
        P(("groups", "blk"), "dp", None, None, None),
        P(("groups", "blk"), "dp", None, None, None),
        P(("groups", "blk"), "dp", None, None, None),
    )
    return jax.shard_map(shards, mesh=mesh, in_specs=in_specs, out_specs=out_specs, check_vma=False)
```

```python
import functools

import jax
import jax.numpy as jnp
from jax import lax
from jax.experimental import pallas as pl
from jax.experimental.pallas import tpu as pltpu
from jax.sharding import PartitionSpec as P

BLOCK = 128
FF = 16384
F32 = jnp.float32
BF16 = jnp.bfloat16
NN = (((1,), (0,)), ((), ()))
NT = (((1,), (1,)), ((), ()))
TN = (((0,), (0,)), ((), ()))
MIB = 1024 * 1024
LONGEST_RING = 8
PIECES = 2
EARLY_MIB, LATE_MIB, DELTA_MIB, INPUT_MIB, NEAR_MIB = 18, 22, 28, 16, 14
EARLY_COST, LATE_COST, DELTA_COST, INPUT_COST, NEAR_COST = 8, 8, 8, 8, 8


def rotate(x, axis, shift):
    n = lax.axis_size(axis)
    return lax.ppermute(x, axis, [(i, (i + shift) % n) for i in range(n)])


def xor_swap(x, axis, bit):
    return lax.ppermute(x, axis, [(i, i ^ bit) for i in range(lax.axis_size(axis))])


def ring_gather(x, g, axis, hold):
    n = lax.axis_size(axis)
    if n > LONGEST_RING:
        me = lax.axis_index(axis)
        return [
            [own] + [lax.dynamic_index_in_dim(whole, (me - i + n) % n, 0, keepdims=False) for i in range(1, n)]
            for own, whole in ((x, lax.all_gather(x, axis)), (g, lax.all_gather(g, axis)))
        ]
    xs, gs = [x], [g]
    for hop in range(1, n):
        xs.append(rotate(xs[-1], axis, 1))
        gs.append(rotate(after(gs[-1], *hold) if hop == 2 else gs[-1], axis, 1))
    return xs, gs


def after(x, *others):
    return lax.optimization_barrier((x, *others))[0]


class Dims:
    def __init__(self, n_dp, n_blk, cap, tokens, width):
        self.n_dp, self.n_blk, self.cap, self.tokens, self.width = n_dp, n_blk, cap, tokens, width
        self.shard_blocks = width // BLOCK
        self.rows = n_blk * self.shard_blocks
        self.own_rows = self.rows // n_dp
        self.cols = FF // (BLOCK * n_blk)
        self.limit = self.own_rows * self.cols
        self.paired = self.own_rows == self.shard_blocks

    def here(self, meta):
        return meta[0], meta[1]

    def place(self, meta, matrix, owner, slot):
        entry = meta[2 + (matrix * self.n_dp + owner) * self.cap + slot]
        kept = jnp.minimum(entry, self.limit - 1)
        return entry < self.limit, owner * self.own_rows + kept // self.cols, kept % self.cols

    def spread(self, piece_ref, shard, target):
        for b in range(self.shard_blocks):
            target[shard * self.shard_blocks + b] = piece_ref[:, b * BLOCK : (b + 1) * BLOCK]


def block(d, group, matrix, slot):
    return group[0][matrix * d.cap + slot] if len(group) == 1 else group[matrix][slot]


def add_products(d, meta, matrix, owner, group, source, form, acc):
    for s in range(d.cap):
        used, row, col = d.place(meta, matrix, owner, s)
        acc[jnp.where(used, col, d.cols)] += lax.dot_general(
            source[row], block(d, group, matrix, s), form, preferred_element_type=F32
        )


def take_groups(refs, places):
    groups, at = {}, 0
    for j in places:
        size = 3 if j > 1 else 1
        groups[j] = refs[at : at + size]
        at += size
    return groups, refs[at:]


def shard_at(d, me, i):
    return lax.rem(me - i + d.n_blk, d.n_blk)


def spread_all(d, me, refs, target):
    for i, ref in enumerate(refs):
        d.spread(ref, shard_at(d, me, i), target)


def early_kernel(d, meta, own_ref, *refs):
    x_refs, g_refs = refs[: d.n_blk - 2], refs[d.n_blk - 2 : 2 * d.n_blk - 4]
    groups, outs = take_groups(refs[2 * d.n_blk - 4 :], range(d.n_dp))
    gate_acc, up_acc, hidden, xs, gs = outs
    me_blk, me_dp = d.here(meta)
    for acc in (gate_acc, up_acc, hidden):
        acc[...] = jnp.zeros_like(acc)
    if not d.paired:
        return
    spread_all(d, me_blk, (own_ref.at[0], *x_refs), xs)
    spread_all(d, me_blk, (own_ref.at[1], *g_refs), gs)
    for j, group in groups.items():
        owner = me_dp ^ j

        @pl.when(owner != shard_at(d, me_blk, d.n_blk - 1))
        def _():
            add_products(d, meta, 0, owner, group, xs, NN, gate_acc)
            add_products(d, meta, 1, owner, group, xs, NN, up_acc)
            add_products(d, meta, 2, owner, group, gs, NT, hidden)


def when_late(d, meta, owner, work):
    if d.paired:
        pl.when(owner == shard_at(d, meta[0], d.n_blk - 1))(work)
    else:
        work()


def late_kernel(d, meta, own_ref, *refs):
    x_refs, (gate_early, up_early) = refs[: d.n_blk - 1], refs[d.n_blk - 1 : d.n_blk + 1]
    groups, outs = take_groups(refs[d.n_blk + 1 :], range(d.n_dp))
    gate_slope, up_slope, act, xs, gate_acc, up_acc = outs
    me_blk, me_dp = d.here(meta)
    for acc in (gate_acc, up_acc):
        acc[...] = jnp.zeros_like(acc)
    spread_all(d, me_blk, (own_ref.at[0], *x_refs), xs)
    for j, group in groups.items():
        owner = me_dp ^ j

        def work():
            add_products(d, meta, 0, owner, group, xs, NN, gate_acc)
            add_products(d, meta, 1, owner, group, xs, NN, up_acc)

        when_late(d, meta, owner, work)

    def activation(c, _):
        gate, up = gate_early[c] + gate_acc[c], up_early[c] + up_acc[c]
        sig = jax.nn.sigmoid(gate)
        activated = gate * sig
        act[c] = (activated * up).astype(BF16)
        gate_slope[c] = up * sig * (1.0 + gate * (1.0 - sig))
        up_slope[c] = activated
        return 0

    lax.fori_loop(0, d.cols, activation, 0, unroll=4)


def partial_grads(d, j, meta, xs, gs, act, gate_delta, up_delta, out_ref):
    owner = meta[1] ^ j
    for matrix in (2, 0, 1):
        for s in range(d.cap):
            used, row, col = d.place(meta, matrix, owner, s)
            if matrix == 2:
                left, right = act[col], gs[row]
            else:
                left, right = xs[row], (gate_delta, up_delta)[matrix][col]
            product = lax.dot_general(left, right, TN, preferred_element_type=F32)
            out_ref[matrix * d.cap + s] = jnp.where(used, product, 0.0).astype(out_ref.dtype)


def delta_kernel(d, places, meta, own_ref, xs, act, gate_slope, up_slope, hidden, *refs):
    g_refs = refs[: d.n_blk - 1]
    groups, outs = take_groups(refs[d.n_blk - 1 :], range(d.n_dp))
    gate_delta, up_delta, gs = outs[:3]
    part_refs, more = outs[3:-1], outs[-1]
    me_blk, me_dp = d.here(meta)
    more[...] = jnp.zeros_like(more)
    spread_all(d, me_blk, (own_ref.at[1], *g_refs), gs)
    for j, group in groups.items():
        owner = me_dp ^ j
        when_late(d, meta, owner, functools.partial(add_products, d, meta, 2, owner, group, gs, NT, more))

    def deltas(c, _):
        total = hidden[c] + more[c]
        gate_delta[c] = (total * gate_slope[c]).astype(BF16)
        up_delta[c] = (total * up_slope[c]).astype(BF16)
        return 0

    lax.fori_loop(0, d.cols, deltas, 0, unroll=4)
    for j, part_ref in zip(places, part_refs):
        partial_grads(d, j, meta, xs, gs, act, gate_delta, up_delta, part_ref)


def input_kernel(d, shifts, meta, gate_delta, up_delta, *refs):
    groups, outs = take_groups(refs, range(d.n_dp))
    out_refs, acc = outs[:-1], outs[-1]
    me_blk, me_dp = d.here(meta)

    def add_owner(owner, group, first_row):
        for matrix, delta in ((0, gate_delta), (1, up_delta)):
            for s in range(d.cap):
                used, row, col = d.place(meta, matrix, owner, s)
                acc[jnp.where(used, row - first_row, acc.shape[0] - 1)] += lax.dot_general(
                    delta[col], block(d, group, matrix, s), NT, preferred_element_type=F32
                )

    if not d.paired:
        acc[...] = jnp.zeros_like(acc)
        for j, group in groups.items():
            add_owner(me_dp ^ j, group, 0)
    for shift, out_ref in zip(shifts, out_refs):
        shard = lax.rem(me_blk + shift, d.n_blk)
        first_row = shard * d.shard_blocks
        if d.paired:
            acc[...] = jnp.zeros_like(acc)
            for j, group in groups.items():
                pl.when(me_dp ^ j == shard)(functools.partial(add_owner, shard, group, first_row))
        for b in range(d.shard_blocks):
            row = b if d.paired else first_row + b
            out_ref[:, b * BLOCK : (b + 1) * BLOCK] = acc[row].astype(out_ref.dtype)


def partial_kernel(d, places, meta, xs, gs, act, gate_delta, up_delta, *part_refs):
    for j, part_ref in zip(places, part_refs):
        partial_grads(d, j, meta, xs, gs, act, gate_delta, up_delta, part_ref)


class Pieces:
    def __init__(self, refs):
        self.refs, self.size, self.dtype = refs, refs[0].shape[0], refs[0].dtype

    def __setitem__(self, at, value):
        self.refs[at // self.size][at % self.size] = value


def near_kernel(d, meta, xs, gs, act, gate_delta, up_delta, own_ref, *next_refs):
    for j, part_ref in ((1, Pieces(next_refs)), (0, own_ref)):
        partial_grads(d, j, meta, xs, gs, act, gate_delta, up_delta, part_ref)


def call(kernel, outs, scratch, mib, cost, meta, *operands):
    vmem = pl.BlockSpec(memory_space=pltpu.VMEM)
    return pl.pallas_call(
        kernel,
        out_shape=outs,
        in_specs=[pl.BlockSpec(memory_space=pltpu.SMEM)] + [vmem] * len(operands),
        out_specs=[vmem] * len(outs),
        scratch_shapes=scratch,
        compiler_params=pltpu.CompilerParams(vmem_limit_bytes=mib * MIB),
        cost_estimate=pl.CostEstimate(flops=MIB, bytes_accessed=cost * MIB, transcendentals=0),
    )(meta, *operands)


def shards(inputs, out_grad, gate_blocks, up_blocks, down_blocks, gate_slots, up_slots, down_slots):
    n_dp, n_blk = lax.axis_size("dp"), lax.axis_size("blk")
    tokens, width = inputs.shape
    cap = gate_blocks.shape[2]
    d = Dims(n_dp, n_blk, cap, tokens, width)
    where = jnp.stack([lax.axis_index("blk"), lax.axis_index("dp")]).astype(jnp.int32)
    meta = jnp.concatenate([where] + [slots.reshape(-1) for slots in (gate_slots, up_slots, down_slots)])
    own_pair = jnp.stack([inputs, out_grad])

    matrices = [blocks[0, 0] for blocks in (gate_blocks, up_blocks, down_blocks)]
    groups = {0: [jnp.concatenate(matrices)]}
    groups[1] = [xor_swap(groups[0][0], "dp", 1)]
    own = (own_pair, groups[0][0], meta)
    x_pieces, g_pieces = ring_gather(inputs, out_grad, "blk", (*own, *groups[1]))
    bit = 2
    while bit < n_dp:
        for j in range(0, bit, 2):
            gate, up, down = groups[j] if j else matrices
            gate = xor_swap(after(gate, *()), "dp", bit)
            up = xor_swap(after(up, *(own_pair, meta)), "dp", bit)
            down = xor_swap(after(down, *(gate,)), "dp", bit)
            groups[j ^ bit] = [gate, up, down]
        bit *= 2
    for j in range(2, n_dp, 2):
        groups[j + 1] = [xor_swap(after(x, x_pieces[-2]), "dp", 1) for x in groups[j]]

    def grid(count, kind):
        return jax.ShapeDtypeStruct((count, tokens, BLOCK), kind)

    def part(j):
        return jax.ShapeDtypeStruct((3 * cap, BLOCK, BLOCK), BF16 if j % 2 else F32)

    def blocks_at(places):
        return [x for j in places for x in groups[j]]

    everyone = blocks_at(range(n_dp))
    sums = [grid(d.cols + 1, F32)] * 3
    gate_early, up_early, hidden = call(
        functools.partial(early_kernel, d), sums, [pltpu.VMEM((d.rows, tokens, BLOCK), BF16)] * 2, EARLY_MIB, EARLY_COST,
        meta, own_pair, *x_pieces[1:-1], *g_pieces[1:-1], *everyone,
    )
    gate_slope, up_slope, act, xs = call(
        functools.partial(late_kernel, d),
        [grid(d.cols, F32), grid(d.cols, F32), grid(d.cols, BF16), grid(d.rows, BF16)],
        [pltpu.VMEM((d.cols + 1, tokens, BLOCK), F32)] * 2, LATE_MIB, LATE_COST,
        meta, own_pair, *x_pieces[1:], gate_early, up_early, *everyone,
    )
    sent, kept_back = list(range(3, n_dp, 2)), list(range(2, n_dp, 2))
    gate_delta, up_delta, gs, *parts_sent = call(
        functools.partial(delta_kernel, d, sent),
        [grid(d.cols, BF16), grid(d.cols, BF16), grid(d.rows, BF16)] + [part(j) for j in sent],
        [pltpu.VMEM((d.cols + 1, tokens, BLOCK), F32)],
        DELTA_MIB, DELTA_COST, meta, own_pair, xs, act, gate_slope, up_slope, hidden, *g_pieces[1:], *everyone,
    )

    def input_share(shifts, gate_delta):
        return call(
            functools.partial(input_kernel, d, shifts),
            [jax.ShapeDtypeStruct((tokens, width), BF16 if shift else F32) for shift in shifts],
            [pltpu.VMEM(((d.shard_blocks if d.paired else d.rows) + 1, tokens, BLOCK), F32)],
            INPUT_MIB, INPUT_COST, meta, gate_delta, up_delta, *everyone,
        )

    others = [xor_swap(x, "dp", 1) for x in parts_sent]
    middle = n_blk // 2
    far = dict(zip([middle], input_share([middle], gate_delta)))
    parts_kept = call(
        functools.partial(partial_kernel, d, kept_back), [part(j) for j in kept_back], [], NEAR_MIB, NEAR_COST,
        meta, xs, gs, act, after(gate_delta, far[middle]), up_delta,
    )
    relayed = [kept + after(other, *parts_kept).astype(F32) for kept, other in zip(parts_kept, others)]
    rest = [shift for shift in range(1, n_blk) if shift != middle] + [0]
    far.update(zip(rest, input_share(rest, after(gate_delta, *relayed))))
    own = far.pop(0)
    moved = [rotate(piece, "blk", shift) for shift, piece in far.items()]
    part_own, *parts_next = call(
        functools.partial(near_kernel, d),
        [part(0)] + [jax.ShapeDtypeStruct((3 * cap // PIECES, BLOCK, BLOCK), BF16)] * PIECES,
        [], NEAR_MIB, NEAR_COST, meta, xs, gs, act, after(gate_delta, own), up_delta,
    )
    part_own = part_own + jnp.concatenate([xor_swap(piece, "dp", 1) for piece in parts_next]).astype(F32)
    parts = [part_own, *relayed]
    bit = 2
    while bit < n_dp:
        arrived = [xor_swap(parts[j + 1].astype(BF16), "dp", bit) for j in range(0, len(parts), 2)]
        kept = parts[::2]
        bit *= 2
        if bit < n_dp:
            parts = [a + b.astype(F32) for a, b in zip(kept, arrived)]
    grads = [
        (kept[0][m * cap : (m + 1) * cap] + arrived[0][m * cap : (m + 1) * cap].astype(F32))
        .astype(BF16)
        .reshape(1, 1, cap, BLOCK, BLOCK)
        for m in range(3)
    ]
    for piece in moved:
        own = own + piece.astype(F32)
    return own.astype(BF16), *grads


def solution(mesh):
    in_specs = (
        P(("groups", "dp"), "blk"),
        P(("groups", "dp"), "blk"),
        P("blk", "dp", None, None, None),
        P("blk", "dp", None, None, None),
        P("blk", "dp", None, None, None),
        P("blk", None, None),
        P("blk", None, None),
        P("blk", None, None),
    )
    out_specs = (
        P(("groups", "dp"), "blk"),
        P(("groups", "blk"), "dp", None, None, None),
        P(("groups", "blk"), "dp", None, None, None),
        P(("groups", "blk"), "dp", None, None, None),
    )
    return jax.shard_map(shards, mesh=mesh, in_specs=in_specs, out_specs=out_specs, check_vma=False)
```

```python
import functools

import jax
import jax.numpy as jnp
from jax import lax
from jax.experimental import pallas as pl
from jax.experimental.pallas import tpu as pltpu
from jax.sharding import PartitionSpec as P

BLOCK = 128
FF = 16384
F32 = jnp.float32
BF16 = jnp.bfloat16
NN = (((1,), (0,)), ((), ()))
NT = (((1,), (1,)), ((), ()))
TN = (((0,), (0,)), ((), ()))
MIB = 1024 * 1024
LONGEST_RING = 8
PIECES = 2
EARLY_MIB, LATE_MIB, DELTA_MIB, INPUT_MIB, NEAR_MIB = 18, 22, 28, 16, 14
EARLY_COST, LATE_COST, DELTA_COST, INPUT_COST, NEAR_COST = 8, 8, 8, 8, 8


def rotate(x, axis, shift):
    n = lax.axis_size(axis)
    return lax.ppermute(x, axis, [(i, (i + shift) % n) for i in range(n)])


def xor_swap(x, axis, bit):
    return lax.ppermute(x, axis, [(i, i ^ bit) for i in range(lax.axis_size(axis))])


def ring_gather(x, g, axis, hold):
    n = lax.axis_size(axis)
    if n > LONGEST_RING:
        me = lax.axis_index(axis)
        return [
            [own] + [lax.dynamic_index_in_dim(whole, (me - i + n) % n, 0, keepdims=False) for i in range(1, n)]
            for own, whole in ((x, lax.all_gather(x, axis)), (g, lax.all_gather(g, axis)))
        ]
    xs, gs = [x], [g]
    for hop in range(1, n):
        xs.append(rotate(xs[-1], axis, 1))
        gs.append(rotate(after(gs[-1], *hold) if hop == 2 else gs[-1], axis, 1))
    return xs, gs


def after(x, *others):
    return lax.optimization_barrier((x, *others))[0]


class Dims:
    def __init__(self, n_dp, n_blk, cap, tokens, width):
        self.n_dp, self.n_blk, self.cap, self.tokens, self.width = n_dp, n_blk, cap, tokens, width
        self.shard_blocks = width // BLOCK
        self.rows = n_blk * self.shard_blocks
        self.own_rows = self.rows // n_dp
        self.cols = FF // (BLOCK * n_blk)
        self.limit = self.own_rows * self.cols
        self.paired = self.own_rows == self.shard_blocks

    def here(self, meta):
        return meta[0], meta[1]

    def place(self, meta, matrix, owner, slot):
        entry = meta[2 + (matrix * self.n_dp + owner) * self.cap + slot]
        kept = jnp.minimum(entry, self.limit - 1)
        return entry < self.limit, owner * self.own_rows + kept // self.cols, kept % self.cols

    def spread(self, piece_ref, shard, target):
        for b in range(self.shard_blocks):
            target[shard * self.shard_blocks + b] = piece_ref[:, b * BLOCK : (b + 1) * BLOCK]


def block(d, group, matrix, slot):
    return group[0][matrix * d.cap + slot] if len(group) == 1 else group[matrix][slot]


def add_products(d, meta, matrix, owner, group, source, form, acc):
    for s in range(d.cap):
        used, row, col = d.place(meta, matrix, owner, s)
        acc[jnp.where(used, col, d.cols)] += lax.dot_general(
            source[row], block(d, group, matrix, s), form, preferred_element_type=F32
        )


def take_groups(refs, places):
    groups, at = {}, 0
    for j in places:
        size = 3 if j > 1 else 1
        groups[j] = refs[at : at + size]
        at += size
    return groups, refs[at:]


def shard_at(d, me, i):
    return lax.rem(me - i + d.n_blk, d.n_blk)


def spread_all(d, me, refs, target):
    for i, ref in enumerate(refs):
        d.spread(ref, shard_at(d, me, i), target)


def early_kernel(d, meta, own_ref, *refs):
    x_refs, g_refs = refs[: d.n_blk - 2], refs[d.n_blk - 2 : 2 * d.n_blk - 4]
    groups, outs = take_groups(refs[2 * d.n_blk - 4 :], range(d.n_dp))
    gate_acc, up_acc, hidden, xs, gs = outs
    me_blk, me_dp = d.here(meta)
    for acc in (gate_acc, up_acc, hidden):
        acc[...] = jnp.zeros_like(acc)
    if not d.paired:
        return
    spread_all(d, me_blk, (own_ref.at[0], *x_refs), xs)
    spread_all(d, me_blk, (own_ref.at[1], *g_refs), gs)
    for j, group in groups.items():
        owner = me_dp ^ j

        @pl.when(owner != shard_at(d, me_blk, d.n_blk - 1))
        def _():
            add_products(d, meta, 0, owner, group, xs, NN, gate_acc)
            add_products(d, meta, 1, owner, group, xs, NN, up_acc)
            add_products(d, meta, 2, owner, group, gs, NT, hidden)


def when_late(d, meta, owner, work):
    if d.paired:
        pl.when(owner == shard_at(d, meta[0], d.n_blk - 1))(work)
    else:
        work()


def late_kernel(d, meta, own_ref, *refs):
    x_refs, (gate_early, up_early) = refs[: d.n_blk - 1], refs[d.n_blk - 1 : d.n_blk + 1]
    groups, outs = take_groups(refs[d.n_blk + 1 :], range(d.n_dp))
    gate_slope, up_slope, act, xs, gate_acc, up_acc = outs
    me_blk, me_dp = d.here(meta)
    for acc in (gate_acc, up_acc):
        acc[...] = jnp.zeros_like(acc)
    spread_all(d, me_blk, (own_ref.at[0], *x_refs), xs)
    for j, group in groups.items():
        owner = me_dp ^ j

        def work():
            add_products(d, meta, 0, owner, group, xs, NN, gate_acc)
            add_products(d, meta, 1, owner, group, xs, NN, up_acc)

        when_late(d, meta, owner, work)

    def activation(c, _):
        gate, up = gate_early[c] + gate_acc[c], up_early[c] + up_acc[c]
        sig = jax.nn.sigmoid(gate)
        activated = gate * sig
        act[c] = (activated * up).astype(BF16)
        gate_slope[c] = up * sig * (1.0 + gate * (1.0 - sig))
        up_slope[c] = activated
        return 0

    lax.fori_loop(0, d.cols, activation, 0, unroll=4)


def partial_grads(d, j, meta, xs, gs, act, gate_delta, up_delta, out_ref):
    owner = meta[1] ^ j
    for matrix in (2, 0, 1):
        for s in range(d.cap):
            used, row, col = d.place(meta, matrix, owner, s)
            if matrix == 2:
                left, right = act[col], gs[row]
            else:
                left, right = xs[row], (gate_delta, up_delta)[matrix][col]
            product = lax.dot_general(left, right, TN, preferred_element_type=F32)
            out_ref[matrix * d.cap + s] = jnp.where(used, product, 0.0).astype(out_ref.dtype)


def delta_kernel(d, places, meta, own_ref, xs, act, gate_slope, up_slope, hidden, *refs):
    g_refs = refs[: d.n_blk - 1]
    groups, outs = take_groups(refs[d.n_blk - 1 :], range(d.n_dp))
    gate_delta, up_delta, gs = outs[:3]
    part_refs, more = outs[3:-1], outs[-1]
    me_blk, me_dp = d.here(meta)
    more[...] = jnp.zeros_like(more)
    spread_all(d, me_blk, (own_ref.at[1], *g_refs), gs)
    for j, group in groups.items():
        owner = me_dp ^ j
        when_late(d, meta, owner, functools.partial(add_products, d, meta, 2, owner, group, gs, NT, more))

    def deltas(c, _):
        total = hidden[c] + more[c]
        gate_delta[c] = (total * gate_slope[c]).astype(BF16)
        up_delta[c] = (total * up_slope[c]).astype(BF16)
        return 0

    lax.fori_loop(0, d.cols, deltas, 0, unroll=16)
    for j, part_ref in zip(places, part_refs):
        partial_grads(d, j, meta, xs, gs, act, gate_delta, up_delta, part_ref)


def input_kernel(d, shifts, meta, gate_delta, up_delta, *refs):
    groups, outs = take_groups(refs, range(d.n_dp))
    out_refs, acc = outs[:-1], outs[-1]
    me_blk, me_dp = d.here(meta)

    def add_owner(owner, group, first_row):
        for matrix, delta in ((0, gate_delta), (1, up_delta)):
            for s in range(d.cap):
                used, row, col = d.place(meta, matrix, owner, s)
                acc[jnp.where(used, row - first_row, acc.shape[0] - 1)] += lax.dot_general(
                    delta[col], block(d, group, matrix, s), NT, preferred_element_type=F32
                )

    if not d.paired:
        acc[...] = jnp.zeros_like(acc)
        for j, group in groups.items():
            add_owner(me_dp ^ j, group, 0)
    for shift, out_ref in zip(shifts, out_refs):
        shard = lax.rem(me_blk + shift, d.n_blk)
        first_row = shard * d.shard_blocks
        if d.paired:
            acc[...] = jnp.zeros_like(acc)
            for j, group in groups.items():
                pl.when(me_dp ^ j == shard)(functools.partial(add_owner, shard, group, first_row))
        for b in range(d.shard_blocks):
            row = b if d.paired else first_row + b
            out_ref[:, b * BLOCK : (b + 1) * BLOCK] = acc[row].astype(out_ref.dtype)


def partial_kernel(d, places, meta, xs, gs, act, gate_delta, up_delta, *part_refs):
    for j, part_ref in zip(places, part_refs):
        partial_grads(d, j, meta, xs, gs, act, gate_delta, up_delta, part_ref)


class Pieces:
    def __init__(self, refs):
        self.refs, self.size, self.dtype = refs, refs[0].shape[0], refs[0].dtype

    def __setitem__(self, at, value):
        self.refs[at // self.size][at % self.size] = value


def near_kernel(d, meta, xs, gs, act, gate_delta, up_delta, own_ref, *next_refs):
    for j, part_ref in ((1, Pieces(next_refs)), (0, own_ref)):
        partial_grads(d, j, meta, xs, gs, act, gate_delta, up_delta, part_ref)


def call(kernel, outs, scratch, mib, cost, meta, *operands):
    vmem = pl.BlockSpec(memory_space=pltpu.VMEM)
    return pl.pallas_call(
        kernel,
        out_shape=outs,
        in_specs=[pl.BlockSpec(memory_space=pltpu.SMEM)] + [vmem] * len(operands),
        out_specs=[vmem] * len(outs),
        scratch_shapes=scratch,
        compiler_params=pltpu.CompilerParams(vmem_limit_bytes=mib * MIB),
        cost_estimate=pl.CostEstimate(flops=MIB, bytes_accessed=cost * MIB, transcendentals=0),
    )(meta, *operands)


def shards(inputs, out_grad, gate_blocks, up_blocks, down_blocks, gate_slots, up_slots, down_slots):
    n_dp, n_blk = lax.axis_size("dp"), lax.axis_size("blk")
    tokens, width = inputs.shape
    cap = gate_blocks.shape[2]
    d = Dims(n_dp, n_blk, cap, tokens, width)
    where = jnp.stack([lax.axis_index("blk"), lax.axis_index("dp")]).astype(jnp.int32)
    meta = jnp.concatenate([where] + [slots.reshape(-1) for slots in (gate_slots, up_slots, down_slots)])
    own_pair = jnp.stack([inputs, out_grad])

    matrices = [blocks[0, 0] for blocks in (gate_blocks, up_blocks, down_blocks)]
    groups = {0: [jnp.concatenate(matrices)]}
    groups[1] = [xor_swap(groups[0][0], "dp", 1)]
    own = (own_pair, groups[0][0], meta)
    x_pieces, g_pieces = ring_gather(inputs, out_grad, "blk", (*own, *groups[1]))
    bit = 2
    while bit < n_dp:
        for j in range(0, bit, 2):
            gate, up, down = groups[j] if j else matrices
            gate = xor_swap(after(gate, *()), "dp", bit)
            up = xor_swap(after(up, *(own_pair, meta)), "dp", bit)
            down = xor_swap(after(down, *(gate,)), "dp", bit)
            groups[j ^ bit] = [gate, up, down]
        bit *= 2
    for j in range(2, n_dp, 2):
        groups[j + 1] = [xor_swap(after(x, x_pieces[-2]), "dp", 1) for x in groups[j]]

    def grid(count, kind):
        return jax.ShapeDtypeStruct((count, tokens, BLOCK), kind)

    def part(j):
        return jax.ShapeDtypeStruct((3 * cap, BLOCK, BLOCK), BF16 if j % 2 else F32)

    def blocks_at(places):
        return [x for j in places for x in groups[j]]

    everyone = blocks_at(range(n_dp))
    sums = [grid(d.cols + 1, F32)] * 3
    gate_early, up_early, hidden = call(
        functools.partial(early_kernel, d), sums, [pltpu.VMEM((d.rows, tokens, BLOCK), BF16)] * 2, EARLY_MIB, EARLY_COST,
        meta, own_pair, *x_pieces[1:-1], *g_pieces[1:-1], *everyone,
    )
    gate_slope, up_slope, act, xs = call(
        functools.partial(late_kernel, d),
        [grid(d.cols, F32), grid(d.cols, F32), grid(d.cols, BF16), grid(d.rows, BF16)],
        [pltpu.VMEM((d.cols + 1, tokens, BLOCK), F32)] * 2, LATE_MIB, LATE_COST,
        meta, own_pair, *x_pieces[1:], gate_early, up_early, *everyone,
    )
    sent, kept_back = list(range(3, n_dp, 2)), list(range(2, n_dp, 2))
    gate_delta, up_delta, gs, *parts_sent = call(
        functools.partial(delta_kernel, d, sent),
        [grid(d.cols, BF16), grid(d.cols, BF16), grid(d.rows, BF16)] + [part(j) for j in sent],
        [pltpu.VMEM((d.cols + 1, tokens, BLOCK), F32)],
        DELTA_MIB, DELTA_COST, meta, own_pair, xs, act, gate_slope, up_slope, hidden, *g_pieces[1:], *everyone,
    )

    def input_share(shifts, gate_delta):
        return call(
            functools.partial(input_kernel, d, shifts),
            [jax.ShapeDtypeStruct((tokens, width), BF16 if shift else F32) for shift in shifts],
            [pltpu.VMEM(((d.shard_blocks if d.paired else d.rows) + 1, tokens, BLOCK), F32)],
            INPUT_MIB, INPUT_COST, meta, gate_delta, up_delta, *everyone,
        )

    others = [xor_swap(x, "dp", 1) for x in parts_sent]
    middle = n_blk // 2
    far = dict(zip([middle], input_share([middle], gate_delta)))
    parts_kept = call(
        functools.partial(partial_kernel, d, kept_back), [part(j) for j in kept_back], [], NEAR_MIB, NEAR_COST,
        meta, xs, gs, act, after(gate_delta, far[middle]), up_delta,
    )
    relayed = [kept + after(other, *parts_kept).astype(F32) for kept, other in zip(parts_kept, others)]
    rest = [shift for shift in range(1, n_blk) if shift != middle] + [0]
    far.update(zip(rest, input_share(rest, after(gate_delta, *relayed))))
    own = far.pop(0)
    moved = [rotate(piece, "blk", shift) for shift, piece in far.items()]
    part_own, *parts_next = call(
        functools.partial(near_kernel, d),
        [part(0)] + [jax.ShapeDtypeStruct((3 * cap // PIECES, BLOCK, BLOCK), BF16)] * PIECES,
        [], NEAR_MIB, NEAR_COST, meta, xs, gs, act, after(gate_delta, own), up_delta,
    )
    part_own = part_own + jnp.concatenate([xor_swap(piece, "dp", 1) for piece in parts_next]).astype(F32)
    parts = [part_own, *relayed]
    bit = 2
    while bit < n_dp:
        arrived = [xor_swap(parts[j + 1].astype(BF16), "dp", bit) for j in range(0, len(parts), 2)]
        kept = parts[::2]
        bit *= 2
        if bit < n_dp:
            parts = [a + b.astype(F32) for a, b in zip(kept, arrived)]
    grads = [
        (kept[0][m * cap : (m + 1) * cap] + arrived[0][m * cap : (m + 1) * cap].astype(F32))
        .astype(BF16)
        .reshape(1, 1, cap, BLOCK, BLOCK)
        for m in range(3)
    ]
    for piece in moved:
        own = own + piece.astype(F32)
    return own.astype(BF16), *grads


def solution(mesh):
    in_specs = (
        P(("groups", "dp"), "blk"),
        P(("groups", "dp"), "blk"),
        P("blk", "dp", None, None, None),
        P("blk", "dp", None, None, None),
        P("blk", "dp", None, None, None),
        P("blk", None, None),
        P("blk", None, None),
        P("blk", None, None),
    )
    out_specs = (
        P(("groups", "dp"), "blk"),
        P(("groups", "blk"), "dp", None, None, None),
        P(("groups", "blk"), "dp", None, None, None),
        P(("groups", "blk"), "dp", None, None, None),
    )
    return jax.shard_map(shards, mesh=mesh, in_specs=in_specs, out_specs=out_specs, check_vma=False)
```
